32 devices in a mesh: grp: 2 (over x), own: 16 (over z, y, core).
Axes of the slice: x: 2, y: 2, z: 4, core: 2. Of those that a mesh axis runs over, the one named last changes fastest.
Arguments:
- coefficients: bfloat16 [64, 512, 4608], P('own', 'grp'), parts along dimension 1, may hold values from -6 to 6
- rotations: bfloat16 [64, 3342336], P('own'), may hold values from -0.75 to 0.75
- legendre: bfloat16 [256, 512, 512], P('own'), may hold values from -48 to 48, as said below
- degree_slot: int32 [8, 64], replicated, may hold values from 0 to 63, each once within a row
- column_order: int32 [512], P('grp'), parts along dimension 0, may hold values from 0 to 255, each once
Outputs:
- grid_errors: bfloat16 [512, 256, 1024], P('grp', 'own'), parts along dimension 0
The draws below stay inside these ranges and needn't reach their ends.
There are 2 independent parts, one for each index of `grp`. The reference program is written for one: setup_inputs(seed, part) draws one part's arguments, and reference() takes and returns one part's arrays. A program takes and returns all parts, laid end to end along the dimension named above; an argument that names none is the same for every part. Nothing has to cross between parts.
Inputs may be any that keep to these rules, and one draw needn't show every extreme that they name: Each row is a permutation; slot s of class k holds degree 64 * k + degree_slot[k, s]. `column_order`: a permutation of the columns. legendre[t, m, l] is zero where l < m.
All inputs are finite; a program needn't handle non-finite values.
Results may differ from the reference program's by a relative error of at most 0.0062.
Values may be sent and summed in bfloat16 or wider, within the bound.
A program may use at most 192 MiB of HBM per device.

```python
import math
import jax
import jax.numpy as jnp
from jax import lax

SLOTS = 64
CLASSES = 8
NLAT = 256
ORDERS = 512
NLON = 1024
COLUMNS = 256
SLOT_ROWS = 4608
ROT_SLOT = 3342336


def draw_rotations(key, part):
    flat = jnp.arange(ROT_SLOT, dtype=jnp.int32)
    bucket = jnp.zeros((ROT_SLOT,), jnp.int32)
    for upper in range(1, CLASSES):
        limit = 4 * SLOTS * SLOTS * upper * (upper + 1) * (2 * upper + 1) // 6
        bucket = bucket + (flat >= limit).astype(jnp.int32)
    spread = 1.0 / jnp.sqrt((2 * SLOTS * (bucket + 1) - SLOTS).astype(jnp.float32))
    values = jax.random.truncated_normal(key, -6.0, 6.0, (SLOTS, ROT_SLOT), jnp.float32)
    return (values * spread[None, :]).astype(jnp.bfloat16)


def legendre_table(colatitude):
    orders = SLOTS * CLASSES
    order_float = jnp.arange(orders, dtype=jnp.float32)
    sines = jnp.sin(colatitude)
    cosines = jnp.cos(colatitude)
    growth = 0.5 * jnp.log((2.0 * order_float + 1.0) / jnp.maximum(2.0 * order_float, 1.0))
    doubling = jnp.where(order_float >= 1.0, 0.5 * math.log(2.0), 0.0)
    log_seed = (jnp.cumsum(growth) + doubling)[:, None] + order_float[:, None] * jnp.log(sines)[None, :]
    seeds = jnp.exp(log_seed)
    squared = order_float * order_float

    def advance(carry, degree):
        previous, earlier = carry
        degree_float = degree.astype(jnp.float32)
        above = degree_float > order_float
        deeper = degree_float > order_float + 1.0
        leading = jnp.sqrt(jnp.where(above, (4.0 * degree_float * degree_float - 1.0) / jnp.where(above, degree_float * degree_float - squared, 1.0), 0.0))
        lowered = degree_float - 1.0
        trailing = jnp.sqrt(jnp.where(deeper, (lowered * lowered - squared) / jnp.where(deeper, 4.0 * lowered * lowered - 1.0, 1.0), 0.0))
        recursed = leading[:, None] * (cosines[None, :] * previous - trailing[:, None] * earlier)
        current = jnp.where(above[:, None], recursed, jnp.where((degree_float == order_float)[:, None], seeds, 0.0))
        return ((current, previous), current)
    initial = jnp.zeros((orders, colatitude.shape[0]), jnp.float32)
    final, values = lax.scan(advance, (initial, initial), jnp.arange(orders, dtype=jnp.int32))
    return jnp.transpose(values, (2, 1, 0))


def draw_legendre(key, part):
    colatitude = jax.random.uniform(key, (NLAT,), jnp.float32, 0.15, math.pi - 0.15)
    return legendre_table(colatitude).astype(jnp.bfloat16)


def steps_of(key, shape, cuts, smallest, largest):
    gain = 1.0
    for dim, blocks in cuts:
        heights = jax.random.uniform(jax.random.fold_in(jax.random.fold_in(key, 6), dim), (blocks,), jnp.float32, smallest / len(cuts), largest / len(cuts))
        gain = gain * jnp.repeat(jnp.exp(heights), shape[dim] // blocks).reshape((-1,) + (1,) * (len(shape) - 1 - dim))
    return gain


def normal_values(own_key, dims, width, most, split=(), held_as=jnp.bfloat16):
    loudness = steps_of(own_key, dims, split, -0.22, 0.18) if split else 1.0
    drawn = jax.random.normal(own_key, dims, jnp.float32) * width * loudness
    return jnp.minimum(jnp.maximum(drawn, -most), most).astype(held_as)


def setup_inputs(seed: int = 0, part: int = 0) -> dict:
    arg_keys = jax.random.split(jax.random.key(seed), 6)
    own_keys = jax.random.split(jax.random.fold_in(arg_keys[5], part), 6)
    coefficients = normal_values(own_keys[0], (SLOTS, COLUMNS, SLOT_ROWS), 1.0, 6.0, ((0, 16),))
    rotations = draw_rotations(jax.random.fold_in(arg_keys[5], 71), part)
    legendre = draw_legendre(jax.random.fold_in(arg_keys[5], 71), part)
    degree_slot = jax.vmap(lambda own: jax.random.permutation(own, SLOTS))(jax.random.split(arg_keys[3], CLASSES)).reshape((CLASSES, SLOTS)).astype(jnp.int32)
    column_order = jax.random.permutation(own_keys[4], COLUMNS).astype(jnp.int32)
    return {"coefficients": coefficients, "rotations": rotations, "legendre": legendre, "degree_slot": degree_slot, "column_order": column_order}


def rotate_bucket(selected, rotations, degrees, bucket):
    extent = 2 * SLOTS * (bucket + 1)
    first_row = SLOTS * bucket * (bucket + 1)
    offset = 4 * SLOTS * SLOTS * bucket * (bucket + 1) * (2 * bucket + 1) // 6
    block = selected[:, :, first_row:first_row + extent].astype(jnp.float32)
    active = jnp.arange(extent, dtype=jnp.int32)[None, :] < (2 * degrees + 1)[:, None]
    block = jnp.where(active[:, None, :], block, jnp.zeros((), jnp.float32))
    matrix = rotations[:, offset:offset + extent * extent].reshape(SLOTS, extent, extent).astype(jnp.float32)
    turned = jnp.einsum("sij,scj->sic", matrix, block)
    return turned.astype(jnp.bfloat16)


def order_entries(turned, degrees, order_ids):
    extent = turned.shape[1]
    upward = degrees[:, None] + order_ids[None, :]
    downward = degrees[:, None] - order_ids[None, :]
    upward_valid = order_ids[None, :] <= degrees[:, None]
    downward_valid = upward_valid & (order_ids[None, :] >= 1)
    cosine = jnp.take_along_axis(turned, jnp.clip(upward, 0, extent - 1)[:, :, None], axis=1)
    sine_part = jnp.take_along_axis(turned, jnp.clip(downward, 0, extent - 1)[:, :, None], axis=1)
    nothing = jnp.zeros((), turned.dtype)
    cosine = jnp.where(upward_valid[:, :, None], cosine, nothing)
    sine_part = jnp.where(downward_valid[:, :, None], sine_part, nothing)
    return jnp.stack([cosine, sine_part], axis=2)


def synthesize_order(inputs):
    legendre_rows, coefficient_rows = inputs
    return jnp.dot(legendre_rows, coefficient_rows, preferred_element_type=jnp.float32).astype(jnp.bfloat16)


def reference(coefficients, rotations, legendre, degree_slot, column_order):
    selected = jnp.take(coefficients, column_order, axis=1)
    order_ids = jnp.arange(ORDERS, dtype=jnp.int32)
    pieces = []
    degree_lists = []
    for bucket in range(CLASSES):
        degrees = (SLOTS * bucket + degree_slot[bucket]).astype(jnp.int32)
        degree_lists.append(degrees)
        turned = rotate_bucket(selected, rotations, degrees, bucket)
        pieces.append(order_entries(turned, degrees, order_ids))
    stacked = jnp.concatenate(pieces, axis=0)
    by_order = jnp.transpose(stacked, (1, 0, 2, 3)).reshape(ORDERS, CLASSES * SLOTS, 2 * COLUMNS)
    degree_index = jnp.concatenate(degree_lists).astype(jnp.int32)
    legendre_slots = jnp.take(legendre, degree_index, axis=2)
    legendre_orders = jnp.transpose(legendre_slots, (1, 0, 2))
    fourier = lax.map(synthesize_order, (legendre_orders, by_order))
    fourier = fourier.reshape(ORDERS, NLAT, 2, COLUMNS)
    fourier = jnp.transpose(fourier, (1, 0, 2, 3)).reshape(NLAT, 2 * ORDERS, COLUMNS)
    longitude = jnp.arange(NLON, dtype=jnp.int32)
    product_mod = (order_ids[:, None] * longitude[None, :]) % NLON
    angles = product_mod.astype(jnp.float32) * (2.0 * math.pi / NLON)
    wave = (jnp.stack([jnp.cos(angles), jnp.sin(angles)], axis=1) / ORDERS).astype(jnp.bfloat16)
    wave = wave.reshape(2 * ORDERS, NLON)

    def transform_latitude(rows):
        return jnp.dot(rows.T, wave, preferred_element_type=jnp.float32).astype(jnp.bfloat16)

    grid = lax.map(transform_latitude, fourier)
    return jnp.transpose(grid, (1, 0, 2))
```

```python
import math

import jax
import jax.numpy as jnp
import numpy as np
from jax import lax
from jax.experimental import pallas as pl
from jax.experimental.pallas import tpu as pltpu
from jax.sharding import PartitionSpec as P

VMEM_BYTES = 56 * 1024 * 1024


def class_extent(bucket, slot_count):
    return 2 * slot_count * (bucket + 1)


def class_first(bucket, slot_count):
    return slot_count * bucket * (bucket + 1)


def class_offset(bucket, slot_count):
    return 4 * slot_count * slot_count * bucket * (bucket + 1) * (2 * bucket + 1) // 6


def signed_orders(bucket, slot_count, owners):
    share = slot_count // owners
    owner, block, inner, part = np.meshgrid(
        np.arange(owners), np.arange(bucket + 1), np.arange(share), np.arange(2), indexing="ij"
    )
    order = slot_count * block + share * owner + inner
    signed = np.where(part == 0, order, -order)
    signed = np.where((part == 1) & (order == 0), 1 << 20, signed)
    return signed.reshape(-1, 1).astype(np.int32)


def rotate_classes(coefficients, rotations, degrees, column_pick, classes, slot_count, owners):
    slot_local, columns, slot_rows = coefficients.shape
    extents = [class_extent(k, slot_count) for k in classes]
    count = len(classes)

    def kernel(degree_ref, coef_ref, pick_ref, *refs):
        matrices, orders, outs = refs[:count], refs[count : 2 * count], refs[2 * count :]
        slot = pl.program_id(0)
        for index, bucket in enumerate(classes):
            extent = extents[index]
            degree = degree_ref[bucket, slot]
            first = class_first(bucket, slot_count)
            block = coef_ref[0, :, first : first + extent]
            lanes = lax.broadcasted_iota(jnp.int32, block.shape, 1)
            block = jnp.where(lanes <= 2 * degree, block, jnp.zeros((), block.dtype))
            turned = lax.dot_general(
                matrices[index][0], block, (((1,), (1,)), ((), ())), preferred_element_type=jnp.float32
            ).astype(jnp.bfloat16)
            turned = jnp.dot(turned, pick_ref[...], preferred_element_type=jnp.float32).astype(jnp.bfloat16)
            target = degree + orders[index][...]
            target = jnp.where(target <= 2 * degree, target, -1)
            rows = lax.broadcasted_iota(jnp.int32, (extent, extent), 1)
            picker = (rows == target).astype(jnp.float32).astype(jnp.bfloat16)
            outs[index][0] = jnp.dot(picker, turned, preferred_element_type=jnp.float32).astype(jnp.bfloat16)

    matrices, orders = [], []
    for bucket, extent in zip(classes, extents):
        offset = class_offset(bucket, slot_count)
        matrices.append(
            rotations[:, offset : offset + extent * extent].reshape(slot_local, extent, extent)
        )
        orders.append(jnp.asarray(signed_orders(bucket, slot_count, owners)))
    by_slot = lambda s, _: (s, 0, 0)
    fixed = lambda s, _: (0, 0)
    return pl.pallas_call(
        kernel,
        grid_spec=pltpu.PrefetchScalarGridSpec(
            num_scalar_prefetch=1,
            grid=(slot_local,),
            in_specs=[
                pl.BlockSpec((1, columns, slot_rows), by_slot),
                pl.BlockSpec((columns, columns), fixed),
                *[pl.BlockSpec((1, n, n), by_slot) for n in extents],
                *[pl.BlockSpec((n, 1), fixed) for n in extents],
            ],
            out_specs=[pl.BlockSpec((1, n, columns), by_slot) for n in extents],
        ),
        out_shape=[jax.ShapeDtypeStruct((slot_local, n, columns), jnp.bfloat16) for n in extents],
        compiler_params=pltpu.CompilerParams(vmem_limit_bytes=VMEM_BYTES),
        cost_estimate=pl.CostEstimate(
            flops=4 * slot_local * columns * sum(n * n for n in extents),
            bytes_accessed=2 * slot_local * sum(n * n + 2 * n * columns for n in extents),
            transcendentals=0,
        ),
    )(degrees, coefficients, column_pick, *matrices, *orders)


def transform(parts, tables):
    owners, latitudes, _, columns = parts[0].shape
    longitudes = tables[0].shape[1]
    if any(part.shape[2] % 16 for part in parts):
        grid = sum(
            jnp.einsum(
                "otrc,orn->ctn",
                part,
                table.reshape(owners, part.shape[2], longitudes),
                preferred_element_type=jnp.float32,
            )
            for part, table in zip(parts, tables)
        )
        return grid.astype(jnp.bfloat16)
    count = len(parts)
    width = 128
    tiles = longitudes // 128

    def kernel(*refs):
        part_refs, table_refs, out_ref, total = refs[:count], refs[count : 2 * count], refs[-2], refs[-1]
        for t in range(latitudes):
            value = None
            for part_ref, table_ref in zip(part_refs, table_refs):
                rows = part_ref[:, t].reshape(table_ref.shape[0], width)
                term = lax.dot_general(
                    rows, table_ref[...], (((0,), (0,)), ((), ())), preferred_element_type=jnp.float32
                )
                value = term if value is None else value + term
            for tile in range(tiles):
                total[pl.ds(tile * width * latitudes + t, width, stride=latitudes), :] = value[
                    :, tile * 128 : (tile + 1) * 128
                ]
        for tile in range(tiles):
            out_ref[:, :, tile * 128 : (tile + 1) * 128] = (
                total[tile * width * latitudes : (tile + 1) * width * latitudes, :]
                .reshape(width, latitudes, 128)
                .astype(jnp.bfloat16)
            )

    return pl.pallas_call(
        kernel,
        grid=(columns // width,),
        in_specs=[
            *[pl.BlockSpec((owners, latitudes, part.shape[2], width), lambda c: (0, 0, 0, c)) for part in parts],
            *[pl.BlockSpec(table.shape, lambda c: (0, 0)) for table in tables],
        ],
        out_specs=pl.BlockSpec((width, latitudes, longitudes), lambda c: (c, 0, 0)),
        out_shape=jax.ShapeDtypeStruct((columns, latitudes, longitudes), jnp.bfloat16),
        scratch_shapes=[pltpu.VMEM((tiles * width * latitudes, 128), jnp.float32)],
        compiler_params=pltpu.CompilerParams(vmem_limit_bytes=VMEM_BYTES),
    )(*parts, *tables)


def local(coefficients, rotations, legendre, degree_slot, column_order):
    owners = lax.axis_size("own")
    groups = lax.axis_size("grp")
    own_index = lax.axis_index("own")
    slot_local, columns, _ = coefficients.shape
    buckets, slot_count = degree_slot.shape
    orders = slot_count * buckets
    longitudes = 2 * orders
    latitudes = legendre.shape[0]
    share = slot_count // owners

    shared = latitudes % groups == 0
    mine = legendre
    if shared:
        mine = lax.dynamic_slice_in_dim(
            legendre, lax.axis_index("grp") * (latitudes // groups), latitudes // groups, axis=0
        )
    mine = mine.reshape(mine.shape[0], buckets, owners, share, orders)
    packed = jnp.concatenate([mine[:, b, :, :, slot_count * b :] for b in range(buckets)], axis=-1)
    lanes = packed.shape[-1]
    packed = packed.transpose(1, 0, 2, 3).reshape(owners, -1, lanes)
    moved = lax.all_to_all(packed, "own", split_axis=0, concat_axis=0, tiled=True)

    degrees = lax.dynamic_slice_in_dim(degree_slot, own_index * slot_local, slot_local, axis=1)
    degrees = degrees + slot_count * jnp.arange(buckets, dtype=jnp.int32)[:, None]
    column_ids = jnp.arange(columns, dtype=jnp.int32)
    column_pick = (column_ids[:, None] == column_order[None, :]).astype(jnp.bfloat16)

    high = buckets - buckets // 4
    chunks = [list(range(buckets - 1, high - 1, -1)), list(range(high - 1, -1, -1))]
    received = {}
    for classes in chunks:
        rotated = rotate_classes(
            coefficients, rotations, degrees, column_pick, classes, slot_count, owners
        )
        outgoing = jnp.concatenate(
            [part.reshape(slot_local, owners, -1, columns) for part in rotated], axis=2
        ).transpose(1, 0, 2, 3)
        arrived = lax.all_to_all(outgoing, "own", split_axis=0, concat_axis=0, tiled=True)
        arrived = arrived.reshape(owners * slot_local, -1, columns)
        start = 0
        for bucket in classes:
            size = (bucket + 1) * share * 2
            received[bucket] = arrived[:, start : start + size].reshape(
                owners * slot_local, bucket + 1, share, 2, columns
            )
            start += size

    if shared:
        moved = lax.all_gather(moved, "grp", axis=0, tiled=False)
        moved = moved.reshape(groups, owners, latitudes // groups, share, lanes)
        moved = moved.transpose(1, 0, 2, 3, 4)
    moved = moved.reshape(owners * latitudes, share, lanes)
    degree_ids = jnp.arange(slot_count, dtype=jnp.int32)
    permuters = (degree_ids[None, :, None] == degree_slot[:, None, :]).astype(jnp.bfloat16)

    def synthesize(blocks):
        pieces = []
        for block in blocks:
            start = slot_count * (block * buckets - block * (block - 1) // 2)
            count = buckets - block
            rows = moved[:, :, start : start + slot_count * count]
            rows = rows.reshape(owners * latitudes, share, count, slot_count)
            rows = jnp.einsum(
                "tikl,kls->tiks", rows, permuters[block:], preferred_element_type=jnp.float32
            ).astype(jnp.bfloat16)
            values = jnp.stack([received[k][:, block] for k in range(block, buckets)], axis=0)
            summed = jnp.einsum("tiks,ksipc->tipc", rows, values, preferred_element_type=jnp.float32)
            pieces.append(summed.astype(jnp.bfloat16).reshape(owners, latitudes, share * 2, columns))
        outgoing = jnp.concatenate(pieces, axis=2)
        return lax.all_to_all(outgoing, "own", split_axis=0, concat_axis=0, tiled=True)

    longitude = jnp.arange(longitudes, dtype=jnp.int32)
    low = buckets // 4
    groups_of_blocks = [
        list(range(high, buckets)),
        list(range(low, high)),
        list(range(low)),
    ]
    parts, tables = [], []
    for blocks in groups_of_blocks:
        parts.append(synthesize(blocks))
        held = (
            slot_count * jnp.asarray(blocks, jnp.int32)[None, :, None]
            + share * jnp.arange(owners, dtype=jnp.int32)[:, None, None]
            + jnp.arange(share, dtype=jnp.int32)[None, None, :]
        ).reshape(-1)
        product_mod = held[:, None] * longitude[None, :] % longitudes
        angles = product_mod.astype(jnp.float32) * (2.0 * math.pi / longitudes)
        table = jnp.stack([jnp.cos(angles), jnp.sin(angles)], axis=1) / orders
        tables.append(table.astype(jnp.bfloat16).reshape(-1, longitudes))
    return transform(parts, tables)


def solution(mesh):
    placed = (P("own", "grp", None), P("own", None), P("own", None, None), P(), P("grp"))
    return jax.shard_map(
        local, mesh=mesh, in_specs=placed, out_specs=P("grp", "own", None), check_vma=False
    )
```

```python
import math

import jax
import jax.numpy as jnp
import numpy as np
from jax import lax
from jax.experimental import pallas as pl
from jax.experimental.pallas import tpu as pltpu
from jax.sharding import PartitionSpec as P

VMEM_BYTES = 56 * 1024 * 1024


def class_extent(bucket, slot_count):
    return 2 * slot_count * (bucket + 1)


def class_first(bucket, slot_count):
    return slot_count * bucket * (bucket + 1)


def class_offset(bucket, slot_count):
    return 4 * slot_count * slot_count * bucket * (bucket + 1) * (2 * bucket + 1) // 6


def signed_orders(bucket, slot_count, owners):
    share = slot_count // owners
    owner, block, inner, part = np.meshgrid(
        np.arange(owners), np.arange(bucket + 1), np.arange(share), np.arange(2), indexing="ij"
    )
    order = slot_count * block + share * owner + inner
    signed = np.where(part == 0, order, -order)
    signed = np.where((part == 1) & (order == 0), 1 << 20, signed)
    return signed.reshape(-1, 1).astype(np.int32)


def rotate_classes(coefficients, rotations, degrees, column_pick, classes, slot_count, owners):
    slot_local, columns, slot_rows = coefficients.shape
    extents = [class_extent(k, slot_count) for k in classes]
    count = len(classes)

    def kernel(degree_ref, coef_ref, pick_ref, *refs):
        matrices, orders, outs = refs[:count], refs[count : 2 * count], refs[2 * count :]
        slot = pl.program_id(0)
        for index, bucket in enumerate(classes):
            extent = extents[index]
            degree = degree_ref[bucket, slot]
            first = class_first(bucket, slot_count)
            block = coef_ref[0, :, first : first + extent]
            lanes = lax.broadcasted_iota(jnp.int32, block.shape, 1)
            block = jnp.where(lanes <= 2 * degree, block, jnp.zeros((), block.dtype))
            turned = lax.dot_general(
                matrices[index][0], block, (((1,), (1,)), ((), ())), preferred_element_type=jnp.float32
            ).astype(jnp.bfloat16)
            turned = jnp.dot(turned, pick_ref[...], preferred_element_type=jnp.float32).astype(jnp.bfloat16)
            target = degree + orders[index][...]
            target = jnp.where(target <= 2 * degree, target, -1)
            rows = lax.broadcasted_iota(jnp.int32, (extent, extent), 1)
            picker = (rows == target).astype(jnp.float32).astype(jnp.bfloat16)
            outs[index][0] = jnp.dot(picker, turned, preferred_element_type=jnp.float32).astype(jnp.bfloat16)

    matrices, orders = [], []
    for bucket, extent in zip(classes, extents):
        offset = class_offset(bucket, slot_count)
        matrices.append(
            rotations[:, offset : offset + extent * extent].reshape(slot_local, extent, extent)
        )
        orders.append(jnp.asarray(signed_orders(bucket, slot_count, owners)))
    by_slot = lambda s, _: (s, 0, 0)
    fixed = lambda s, _: (0, 0)
    return pl.pallas_call(
        kernel,
        grid_spec=pltpu.PrefetchScalarGridSpec(
            num_scalar_prefetch=1,
            grid=(slot_local,),
            in_specs=[
                pl.BlockSpec((1, columns, slot_rows), by_slot),
                pl.BlockSpec((columns, columns), fixed),
                *[pl.BlockSpec((1, n, n), by_slot) for n in extents],
                *[pl.BlockSpec((n, 1), fixed) for n in extents],
            ],
            out_specs=[pl.BlockSpec((1, n, columns), by_slot) for n in extents],
        ),
        out_shape=[jax.ShapeDtypeStruct((slot_local, n, columns), jnp.bfloat16) for n in extents],
        compiler_params=pltpu.CompilerParams(vmem_limit_bytes=VMEM_BYTES),
        cost_estimate=pl.CostEstimate(
            flops=4 * slot_local * columns * sum(n * n for n in extents),
            bytes_accessed=2 * slot_local * sum(n * n + 2 * n * columns for n in extents),
            transcendentals=0,
        ),
    )(degrees, coefficients, column_pick, *matrices, *orders)


def transform(parts, tables):
    owners, latitudes, _, columns = parts[0].shape
    longitudes = tables[0].shape[1]
    if any(part.shape[2] % 16 for part in parts):
        grid = sum(
            jnp.einsum(
                "otrc,orn->ctn",
                part,
                table.reshape(owners, part.shape[2], longitudes),
                preferred_element_type=jnp.float32,
            )
            for part, table in zip(parts, tables)
        )
        return grid.astype(jnp.bfloat16)
    width = 256

    def term(part_ref, table_ref, t):
        rows = part_ref[:, t].reshape(table_ref.shape[0], columns)
        return lax.dot_general(
            rows, table_ref[...], (((0,), (0,)), ((), ())), preferred_element_type=jnp.float32
        )

    def early(*refs):
        half = len(refs) // 2
        for t in range(latitudes):
            value = term(refs[0], refs[half], t)
            for part_ref, table_ref in zip(refs[1:half], refs[half + 1 : -1]):
                value = value + term(part_ref, table_ref, t)
            refs[-1][t] = value

    def late(part_ref, table_ref, sum_ref, out_ref, total):
        size = columns * latitudes
        for t in range(latitudes):
            value = sum_ref[t] + term(part_ref, table_ref, t)
            for tile in range(width // 128):
                total[pl.ds(tile * size + t, columns, stride=latitudes), :] = value[
                    :, tile * 128 : (tile + 1) * 128
                ]
        for tile in range(width // 128):
            out_ref[:, :, tile * 128 : (tile + 1) * 128] = (
                total[tile * size : (tile + 1) * size, :]
                .reshape(columns, latitudes, 128)
                .astype(jnp.bfloat16)
            )

    def part_spec(part):
        return pl.BlockSpec(part.shape, lambda n: (0, 0, 0, 0))

    def table_spec(table):
        return pl.BlockSpec((table.shape[0], width), lambda n: (0, n))

    sum_spec = pl.BlockSpec((latitudes, columns, width), lambda n: (0, 0, n))
    params = pltpu.CompilerParams(vmem_limit_bytes=VMEM_BYTES)
    partial = pl.pallas_call(
        early,
        grid=(longitudes // width,),
        in_specs=[*map(part_spec, parts[:-1]), *map(table_spec, tables[:-1])],
        out_specs=sum_spec,
        out_shape=jax.ShapeDtypeStruct((latitudes, columns, longitudes), jnp.float32),
        compiler_params=params,
        cost_estimate=pl.CostEstimate(
            flops=2 * latitudes * columns * longitudes * sum(t.shape[0] for t in tables[:-1]),
            bytes_accessed=4 * latitudes * columns * longitudes,
            transcendentals=0,
        ),
    )(*parts[:-1], *tables[:-1])
    return pl.pallas_call(
        late,
        grid=(longitudes // width,),
        in_specs=[part_spec(parts[-1]), table_spec(tables[-1]), sum_spec],
        out_specs=pl.BlockSpec((columns, latitudes, width), lambda n: (0, 0, n)),
        out_shape=jax.ShapeDtypeStruct((columns, latitudes, longitudes), jnp.bfloat16),
        scratch_shapes=[pltpu.VMEM((width // 128 * columns * latitudes, 128), jnp.float32)],
        compiler_params=params,
    )(parts[-1], tables[-1], partial)


def local(coefficients, rotations, legendre, degree_slot, column_order):
    owners = lax.axis_size("own")
    groups = lax.axis_size("grp")
    own_index = lax.axis_index("own")
    slot_local, columns, _ = coefficients.shape
    buckets, slot_count = degree_slot.shape
    orders = slot_count * buckets
    longitudes = 2 * orders
    latitudes = legendre.shape[0]
    share = slot_count // owners

    shared = latitudes % groups == 0
    mine = legendre
    if shared:
        mine = lax.dynamic_slice_in_dim(
            legendre, lax.axis_index("grp") * (latitudes // groups), latitudes // groups, axis=0
        )
    mine = mine.reshape(mine.shape[0], buckets, owners, share, orders).transpose(2, 0, 3, 1, 4)
    mine = mine.reshape(owners, -1, buckets * orders)
    packed = jnp.concatenate(
        [mine[:, :, orders * b + slot_count * b : orders * (b + 1)] for b in range(buckets)], axis=-1
    )
    lanes = packed.shape[-1]
    moved = lax.all_to_all(packed, "own", split_axis=0, concat_axis=0, tiled=True)

    degrees = lax.dynamic_slice_in_dim(degree_slot, own_index * slot_local, slot_local, axis=1)
    degrees = degrees + slot_count * jnp.arange(buckets, dtype=jnp.int32)[:, None]
    column_ids = jnp.arange(columns, dtype=jnp.int32)
    column_pick = (column_ids[:, None] == column_order[None, :]).astype(jnp.bfloat16)

    high = buckets - buckets // 4
    chunks = [list(range(buckets - 1, high - 1, -1)), list(range(high - 1, -1, -1))]
    received = {}
    for classes in chunks:
        rotated = rotate_classes(
            coefficients, rotations, degrees, column_pick, classes, slot_count, owners
        )
        outgoing = jnp.concatenate(
            [part.reshape(slot_local, owners, -1, columns) for part in rotated], axis=2
        ).transpose(1, 0, 2, 3)
        arrived = lax.all_to_all(outgoing, "own", split_axis=0, concat_axis=0, tiled=True)
        arrived = arrived.reshape(owners * slot_local, -1, columns)
        start = 0
        for bucket in classes:
            size = (bucket + 1) * share * 2
            received[bucket] = arrived[:, start : start + size].reshape(
                owners * slot_local, bucket + 1, share, 2, columns
            )
            start += size

    if shared:
        moved = lax.all_gather(moved, "grp", axis=0, tiled=False)
        moved = moved.reshape(groups, owners, latitudes // groups, share, lanes)
        moved = moved.transpose(1, 0, 2, 3, 4)
    moved = moved.reshape(owners * latitudes, share, lanes)
    degree_ids = jnp.arange(slot_count, dtype=jnp.int32)
    permuters = (degree_ids[None, :, None] == degree_slot[:, None, :]).astype(jnp.bfloat16)

    def synthesize(blocks, received, after):
        pieces = []
        if after is not None:
            received, _ = lax.optimization_barrier((received, after))
        for block in blocks:
            start = slot_count * (block * buckets - block * (block - 1) // 2)
            count = buckets - block
            rows = moved[:, :, start : start + slot_count * count]
            rows = rows.reshape(owners * latitudes, share, count, slot_count)
            rows = jnp.einsum(
                "tikl,kls->tiks", rows, permuters[block:], preferred_element_type=jnp.float32
            ).astype(jnp.bfloat16)
            values = jnp.stack([received[k][:, block] for k in range(block, buckets)], axis=0)
            summed = jnp.einsum("tiks,ksipc->tipc", rows, values, preferred_element_type=jnp.float32)
            pieces.append(summed.astype(jnp.bfloat16).reshape(owners, latitudes, share * 2, columns))
        outgoing = jnp.concatenate(pieces, axis=2)
        return outgoing, lax.all_to_all(outgoing, "own", split_axis=0, concat_axis=0, tiled=True)

    longitude = jnp.arange(longitudes, dtype=jnp.int32)
    low = buckets // 4
    groups_of_blocks = [
        list(range(high, buckets)),
        list(range(low, high)),
        list(range(low)),
    ]
    parts, tables, after = [], [], None
    for blocks in groups_of_blocks:
        after, part = synthesize(blocks, received, after if len(parts) == 2 else None)
        parts.append(part)
        held = (
            slot_count * jnp.asarray(blocks, jnp.int32)[None, :, None]
            + share * jnp.arange(owners, dtype=jnp.int32)[:, None, None]
            + jnp.arange(share, dtype=jnp.int32)[None, None, :]
        ).reshape(-1)
        product_mod = held[:, None] * longitude[None, :] % longitudes
        angles = product_mod.astype(jnp.float32) * (2.0 * math.pi / longitudes)
        table = jnp.stack([jnp.cos(angles), jnp.sin(angles)], axis=1) / orders
        tables.append(table.astype(jnp.bfloat16).reshape(-1, longitudes))
    return transform(parts, tables)


def solution(mesh):
    placed = (P("own", "grp", None), P("own", None), P("own", None, None), P(), P("grp"))
    return jax.shard_map(
        local, mesh=mesh, in_specs=placed, out_specs=P("grp", "own", None), check_vma=False
    )
```

```python
import math

import jax
import jax.numpy as jnp
import numpy as np
from jax import lax
from jax.experimental import pallas as pl
from jax.experimental.pallas import tpu as pltpu
from jax.sharding import PartitionSpec as P

VMEM_BYTES = 56 * 1024 * 1024


def class_extent(bucket, slot_count):
    return 2 * slot_count * (bucket + 1)


def class_first(bucket, slot_count):
    return slot_count * bucket * (bucket + 1)


def class_offset(bucket, slot_count):
    return 4 * slot_count * slot_count * bucket * (bucket + 1) * (2 * bucket + 1) // 6


def signed_orders(bucket, slot_count, owners):
    share = slot_count // owners
    owner, block, inner, part = np.meshgrid(
        np.arange(owners), np.arange(bucket + 1), np.arange(share), np.arange(2), indexing="ij"
    )
    order = slot_count * block + share * owner + inner
    signed = np.where(part == 0, order, -order)
    signed = np.where((part == 1) & (order == 0), 1 << 20, signed)
    return signed.reshape(-1, 1).astype(np.int32)


def rotate_classes(coefficients, rotations, degrees, column_pick, classes, slot_count, owners):
    slot_local, columns, slot_rows = coefficients.shape
    extents = [class_extent(k, slot_count) for k in classes]
    count = len(classes)

    def kernel(degree_ref, coef_ref, pick_ref, *refs):
        matrices, orders, outs = refs[:count], refs[count : 2 * count], refs[2 * count :]
        slot = pl.program_id(0)
        for index, bucket in enumerate(classes):
            extent = extents[index]
            degree = degree_ref[bucket, slot]
            first = class_first(bucket, slot_count)
            block = coef_ref[0, :, first : first + extent]
            lanes = lax.broadcasted_iota(jnp.int32, block.shape, 1)
            block = jnp.where(lanes <= 2 * degree, block, jnp.zeros((), block.dtype))
            turned = lax.dot_general(
                matrices[index][0], block, (((1,), (1,)), ((), ())), preferred_element_type=jnp.float32
            ).astype(jnp.bfloat16)
            turned = jnp.dot(turned, pick_ref[...], preferred_element_type=jnp.float32).astype(jnp.bfloat16)
            target = degree + orders[index][...]
            target = jnp.where(target <= 2 * degree, target, -1)
            rows = lax.broadcasted_iota(jnp.int32, (extent, extent), 1)
            picker = (rows == target).astype(jnp.float32).astype(jnp.bfloat16)
            outs[index][0] = jnp.dot(picker, turned, preferred_element_type=jnp.float32).astype(jnp.bfloat16)

    matrices, orders = [], []
    for bucket, extent in zip(classes, extents):
        offset = class_offset(bucket, slot_count)
        matrices.append(
            rotations[:, offset : offset + extent * extent].reshape(slot_local, extent, extent)
        )
        orders.append(jnp.asarray(signed_orders(bucket, slot_count, owners)))
    by_slot = lambda s, _: (s, 0, 0)
    fixed = lambda s, _: (0, 0)
    return pl.pallas_call(
        kernel,
        grid_spec=pltpu.PrefetchScalarGridSpec(
            num_scalar_prefetch=1,
            grid=(slot_local,),
            in_specs=[
                pl.BlockSpec((1, columns, slot_rows), by_slot),
                pl.BlockSpec((columns, columns), fixed),
                *[pl.BlockSpec((1, n, n), by_slot) for n in extents],
                *[pl.BlockSpec((n, 1), fixed) for n in extents],
            ],
            out_specs=[pl.BlockSpec((1, n, columns), by_slot) for n in extents],
        ),
        out_shape=[jax.ShapeDtypeStruct((slot_local, n, columns), jnp.bfloat16) for n in extents],
        compiler_params=pltpu.CompilerParams(vmem_limit_bytes=VMEM_BYTES),
        cost_estimate=pl.CostEstimate(
            flops=4 * slot_local * columns * sum(n * n for n in extents),
            bytes_accessed=2 * slot_local * sum(n * n + 2 * n * columns for n in extents),
            transcendentals=0,
        ),
    )(degrees, coefficients, column_pick, *matrices, *orders)


def transform(parts, tables):
    owners, latitudes, _, columns = parts[0].shape
    longitudes = tables[0].shape[1]
    if any(part.shape[2] % 16 for part in parts):
        grid = sum(
            jnp.einsum(
                "otrc,orn->ctn",
                part,
                table.reshape(owners, part.shape[2], longitudes),
                preferred_element_type=jnp.float32,
            )
            for part, table in zip(parts, tables)
        )
        return grid.astype(jnp.bfloat16)
    width = 256

    def term(part_ref, table_ref, t):
        rows = part_ref[:, t].reshape(table_ref.shape[0], columns)
        return lax.dot_general(
            rows, table_ref[...], (((0,), (0,)), ((), ())), preferred_element_type=jnp.float32
        )

    def early(*refs):
        half = len(refs) // 2
        for t in range(latitudes):
            value = term(refs[0], refs[half], t)
            for part_ref, table_ref in zip(refs[1:half], refs[half + 1 : -1]):
                value = value + term(part_ref, table_ref, t)
            refs[-1][t] = value

    def late(part_ref, table_ref, sum_ref, out_ref, total):
        size = columns * latitudes
        for t in range(latitudes):
            value = sum_ref[t] + term(part_ref, table_ref, t)
            for tile in range(width // 128):
                total[pl.ds(tile * size + t, columns, stride=latitudes), :] = value[
                    :, tile * 128 : (tile + 1) * 128
                ]
        for tile in range(width // 128):
            out_ref[:, :, tile * 128 : (tile + 1) * 128] = (
                total[tile * size : (tile + 1) * size, :]
                .reshape(columns, latitudes, 128)
                .astype(jnp.bfloat16)
            )

    def part_spec(part):
        return pl.BlockSpec(part.shape, lambda n: (0, 0, 0, 0))

    def table_spec(table):
        return pl.BlockSpec((table.shape[0], width), lambda n: (0, n))

    sum_spec = pl.BlockSpec((latitudes, columns, width), lambda n: (0, 0, n))
    params = pltpu.CompilerParams(vmem_limit_bytes=VMEM_BYTES)
    partial = pl.pallas_call(
        early,
        grid=(longitudes // width,),
        in_specs=[*map(part_spec, parts[:-1]), *map(table_spec, tables[:-1])],
        out_specs=sum_spec,
        out_shape=jax.ShapeDtypeStruct((latitudes, columns, longitudes), jnp.float32),
        compiler_params=params,
        cost_estimate=pl.CostEstimate(
            flops=2 * latitudes * columns * longitudes * sum(t.shape[0] for t in tables[:-1]),
            bytes_accessed=4 * latitudes * columns * longitudes,
            transcendentals=0,
        ),
    )(*parts[:-1], *tables[:-1])
    return pl.pallas_call(
        late,
        grid=(longitudes // width,),
        in_specs=[part_spec(parts[-1]), table_spec(tables[-1]), sum_spec],
        out_specs=pl.BlockSpec((columns, latitudes, width), lambda n: (0, 0, n)),
        out_shape=jax.ShapeDtypeStruct((columns, latitudes, longitudes), jnp.bfloat16),
        scratch_shapes=[pltpu.VMEM((width // 128 * columns * latitudes, 128), jnp.float32)],
        compiler_params=params,
    )(parts[-1], tables[-1], partial)


def local(coefficients, rotations, legendre, degree_slot, column_order):
    owners = lax.axis_size("own")
    groups = lax.axis_size("grp")
    own_index = lax.axis_index("own")
    slot_local, columns, _ = coefficients.shape
    buckets, slot_count = degree_slot.shape
    orders = slot_count * buckets
    longitudes = 2 * orders
    latitudes = legendre.shape[0]
    share = slot_count // owners

    shared = latitudes % groups == 0
    mine = legendre
    if shared:
        mine = lax.dynamic_slice_in_dim(
            legendre, lax.axis_index("grp") * (latitudes // groups), latitudes // groups, axis=0
        )
    mine = mine.reshape(mine.shape[0], buckets, owners, share, orders)
    packed = jnp.concatenate([mine[:, b, :, :, slot_count * b :] for b in range(buckets)], axis=-1)
    lanes = packed.shape[-1]
    packed = packed.transpose(1, 0, 2, 3).reshape(owners, -1, lanes)
    moved = lax.all_to_all(packed, "own", split_axis=0, concat_axis=0, tiled=True)

    degrees = lax.dynamic_slice_in_dim(degree_slot, own_index * slot_local, slot_local, axis=1)
    degrees = degrees + slot_count * jnp.arange(buckets, dtype=jnp.int32)[:, None]
    column_ids = jnp.arange(columns, dtype=jnp.int32)
    column_pick = (column_ids[:, None] == column_order[None, :]).astype(jnp.bfloat16)

    high = buckets - buckets // 4
    chunks = [list(range(buckets - 1, high - 1, -1)), list(range(high - 1, -1, -1))]
    received = {}
    for classes in chunks:
        rotated = rotate_classes(
            coefficients, rotations, degrees, column_pick, classes, slot_count, owners
        )
        outgoing = jnp.concatenate(
            [part.reshape(slot_local, owners, -1, columns) for part in rotated], axis=2
        ).transpose(1, 0, 2, 3)
        degrees, _ = lax.optimization_barrier((degrees, outgoing))
        arrived = lax.all_to_all(outgoing, "own", split_axis=0, concat_axis=0, tiled=True)
        arrived = arrived.reshape(owners * slot_local, -1, columns)
        start = 0
        for bucket in classes:
            size = (bucket + 1) * share * 2
            received[bucket] = arrived[:, start : start + size].reshape(
                owners * slot_local, bucket + 1, share, 2, columns
            )
            start += size

    if shared:
        moved = lax.all_gather(moved, "grp", axis=0, tiled=False)
        moved = moved.reshape(groups, owners, latitudes // groups, share, lanes)
        moved = moved.transpose(1, 0, 2, 3, 4)
    moved = moved.reshape(owners * latitudes, share, lanes)
    held_degrees = degree_slot + slot_count * jnp.arange(buckets, dtype=jnp.int32)[:, None]
    permuter = jnp.arange(orders, dtype=jnp.int32)[:, None] == held_degrees.reshape(1, -1)
    permuter = permuter.astype(jnp.bfloat16)
    tables_of_blocks = []
    for block in range(buckets):
        start = slot_count * (block * buckets - block * (block - 1) // 2)
        first = slot_count * block
        rows = jnp.einsum(
            "til,lj->itj",
            moved[:, :, start : start + orders - first],
            permuter[first:, first:],
            preferred_element_type=jnp.float32,
        )
        tables_of_blocks.append(rows.astype(jnp.bfloat16))
    low_arrived = {k: received[k] for k in chunks[1]}
    low_arrived, tables_of_blocks[:high] = lax.optimization_barrier(
        (low_arrived, tables_of_blocks[:high])
    )

    def synthesize(blocks, received, after):
        pieces = []
        if after is not None:
            received, _ = lax.optimization_barrier((received, after))
        for block in blocks:
            values = jnp.concatenate([received[k][:, block] for k in range(block, buckets)], axis=0)
            summed = jnp.einsum(
                "itj,jipc->tipc", tables_of_blocks[block], values, preferred_element_type=jnp.float32
            )
            pieces.append(summed.astype(jnp.bfloat16).reshape(owners, latitudes, share * 2, columns))
        outgoing = jnp.concatenate(pieces, axis=2)
        return outgoing, lax.all_to_all(outgoing, "own", split_axis=0, concat_axis=0, tiled=True)

    longitude = jnp.arange(longitudes, dtype=jnp.int32)
    low = buckets // 4
    groups_of_blocks = [
        list(range(high, buckets)),
        list(range(low, high)),
        list(range(low)),
    ]
    parts, tables, after = [], [], None
    received = {**received, **low_arrived}
    for blocks in groups_of_blocks:
        after, part = synthesize(blocks, received, after if len(parts) == 2 else None)
        parts.append(part)
        held = (
            slot_count * jnp.asarray(blocks, jnp.int32)[None, :, None]
            + share * jnp.arange(owners, dtype=jnp.int32)[:, None, None]
            + jnp.arange(share, dtype=jnp.int32)[None, None, :]
        ).reshape(-1)
        product_mod = held[:, None] * longitude[None, :] % longitudes
        angles = product_mod.astype(jnp.float32) * (2.0 * math.pi / longitudes)
        table = jnp.stack([jnp.cos(angles), jnp.sin(angles)], axis=1) / orders
        tables.append(table.astype(jnp.bfloat16).reshape(-1, longitudes))
    return transform(parts, tables)


def solution(mesh):
    placed = (P("own", "grp", None), P("own", None), P("own", None, None), P(), P("grp"))
    return jax.shard_map(
        local, mesh=mesh, in_specs=placed, out_specs=P("grp", "own", None), check_vma=False
    )
```

```python
import math

import jax
import jax.numpy as jnp
import numpy as np
from jax import lax
from jax.experimental import pallas as pl
from jax.experimental.pallas import tpu as pltpu
from jax.sharding import PartitionSpec as P

VMEM_BYTES = 56 * 1024 * 1024


def class_extent(bucket, slot_count):
    return 2 * slot_count * (bucket + 1)


def class_first(bucket, slot_count):
    return slot_count * bucket * (bucket + 1)


def class_offset(bucket, slot_count):
    return 4 * slot_count * slot_count * bucket * (bucket + 1) * (2 * bucket + 1) // 6


def signed_orders(bucket, slot_count, owners):
    share = slot_count // owners
    owner, block, inner, part = np.meshgrid(
        np.arange(owners), np.arange(bucket + 1), np.arange(share), np.arange(2), indexing="ij"
    )
    order = slot_count * block + share * owner + inner
    signed = np.where(part == 0, order, -order)
    signed = np.where((part == 1) & (order == 0), 1 << 20, signed)
    return signed.reshape(-1, 1).astype(np.int32)


def rotate_classes(coefficients, rotations, degrees, column_pick, classes, slot_count, owners):
    slot_local, columns, slot_rows = coefficients.shape
    extents = [class_extent(k, slot_count) for k in classes]
    count = len(classes)

    def kernel(degree_ref, coef_ref, pick_ref, *refs):
        matrices, orders, outs = refs[:count], refs[count : 2 * count], refs[2 * count :]
        slot = pl.program_id(0)
        for index, bucket in enumerate(classes):
            extent = extents[index]
            degree = degree_ref[bucket, slot]
            first = class_first(bucket, slot_count)
            block = coef_ref[0, :, first : first + extent]
            lanes = lax.broadcasted_iota(jnp.int32, block.shape, 1)
            block = jnp.where(lanes <= 2 * degree, block, jnp.zeros((), block.dtype))
            turned = lax.dot_general(
                matrices[index][0], block, (((1,), (1,)), ((), ())), preferred_element_type=jnp.float32
            ).astype(jnp.bfloat16)
            turned = jnp.dot(turned, pick_ref[...], preferred_element_type=jnp.float32).astype(jnp.bfloat16)
            target = degree + orders[index][...]
            target = jnp.where(target <= 2 * degree, target, -1)
            rows = lax.broadcasted_iota(jnp.int32, (extent, extent), 1)
            picker = (rows == target).astype(jnp.float32).astype(jnp.bfloat16)
            outs[index][0] = jnp.dot(picker, turned, preferred_element_type=jnp.float32).astype(jnp.bfloat16)

    matrices, orders = [], []
    for bucket, extent in zip(classes, extents):
        offset = class_offset(bucket, slot_count)
        matrices.append(
            rotations[:, offset : offset + extent * extent].reshape(slot_local, extent, extent)
        )
        orders.append(jnp.asarray(signed_orders(bucket, slot_count, owners)))
    by_slot = lambda s, _: (s, 0, 0)
    fixed = lambda s, _: (0, 0)
    return pl.pallas_call(
        kernel,
        grid_spec=pltpu.PrefetchScalarGridSpec(
            num_scalar_prefetch=1,
            grid=(slot_local,),
            in_specs=[
                pl.BlockSpec((1, columns, slot_rows), by_slot),
                pl.BlockSpec((columns, columns), fixed),
                *[pl.BlockSpec((1, n, n), by_slot) for n in extents],
                *[pl.BlockSpec((n, 1), fixed) for n in extents],
            ],
            out_specs=[pl.BlockSpec((1, n, columns), by_slot) for n in extents],
        ),
        out_shape=[jax.ShapeDtypeStruct((slot_local, n, columns), jnp.bfloat16) for n in extents],
        compiler_params=pltpu.CompilerParams(vmem_limit_bytes=VMEM_BYTES),
        cost_estimate=pl.CostEstimate(
            flops=4 * slot_local * columns * sum(n * n for n in extents),
            bytes_accessed=2 * slot_local * sum(n * n + 2 * n * columns for n in extents),
            transcendentals=0,
        ),
    )(degrees, coefficients, column_pick, *matrices, *orders)


def transform(parts, tables):
    owners, latitudes, _, columns = parts[0].shape
    longitudes = tables[0].shape[1]
    if any(part.shape[2] % 16 for part in parts):
        grid = sum(
            jnp.einsum(
                "otrc,orn->ctn",
                part,
                table.reshape(owners, part.shape[2], longitudes),
                preferred_element_type=jnp.float32,
            )
            for part, table in zip(parts, tables)
        )
        return grid.astype(jnp.bfloat16)
    width = 256

    def term(part_ref, table_ref, t):
        rows = part_ref[:, t].reshape(table_ref.shape[0], columns)
        return lax.dot_general(
            rows, table_ref[...], (((0,), (0,)), ((), ())), preferred_element_type=jnp.float32
        )

    def early(*refs):
        half = len(refs) // 2
        for t in range(latitudes):
            value = term(refs[0], refs[half], t)
            for part_ref, table_ref in zip(refs[1:half], refs[half + 1 : -1]):
                value = value + term(part_ref, table_ref, t)
            refs[-1][t] = value

    def late(part_ref, table_ref, sum_ref, out_ref, total):
        size = columns * latitudes
        for t in range(latitudes):
            value = sum_ref[t] + term(part_ref, table_ref, t)
            for tile in range(width // 128):
                total[pl.ds(tile * size + t, columns, stride=latitudes), :] = value[
                    :, tile * 128 : (tile + 1) * 128
                ]
        for tile in range(width // 128):
            out_ref[:, :, tile * 128 : (tile + 1) * 128] = (
                total[tile * size : (tile + 1) * size, :]
                .reshape(columns, latitudes, 128)
                .astype(jnp.bfloat16)
            )

    def part_spec(part):
        return pl.BlockSpec(part.shape, lambda n: (0, 0, 0, 0))

    def table_spec(table):
        return pl.BlockSpec((table.shape[0], width), lambda n: (0, n))

    sum_spec = pl.BlockSpec((latitudes, columns, width), lambda n: (0, 0, n))
    params = pltpu.CompilerParams(vmem_limit_bytes=VMEM_BYTES)
    partial = pl.pallas_call(
        early,
        grid=(longitudes // width,),
        in_specs=[*map(part_spec, parts[:-1]), *map(table_spec, tables[:-1])],
        out_specs=sum_spec,
        out_shape=jax.ShapeDtypeStruct((latitudes, columns, longitudes), jnp.float32),
        compiler_params=params,
        cost_estimate=pl.CostEstimate(
            flops=2 * latitudes * columns * longitudes * sum(t.shape[0] for t in tables[:-1]),
            bytes_accessed=4 * latitudes * columns * longitudes,
            transcendentals=0,
        ),
    )(*parts[:-1], *tables[:-1])
    return pl.pallas_call(
        late,
        grid=(longitudes // width,),
        in_specs=[part_spec(parts[-1]), table_spec(tables[-1]), sum_spec],
        out_specs=pl.BlockSpec((columns, latitudes, width), lambda n: (0, 0, n)),
        out_shape=jax.ShapeDtypeStruct((columns, latitudes, longitudes), jnp.bfloat16),
        scratch_shapes=[pltpu.VMEM((width // 128 * columns * latitudes, 128), jnp.float32)],
        compiler_params=params,
    )(parts[-1], tables[-1], partial)


def pack(legendre, buckets, slot_count, owners, groups):
    share = slot_count // owners
    orders = slot_count * buckets
    latitudes = legendre.shape[0] // groups
    group = lax.axis_index("grp") if groups > 1 else jnp.int32(0)
    starts = [slot_count * (b * buckets - b * (b - 1) // 2) for b in range(buckets + 1)]
    lanes = starts[-1]
    if share % 4:
        mine = lax.dynamic_slice_in_dim(legendre, group * latitudes, latitudes, axis=0)
        mine = mine.reshape(latitudes, buckets, owners, share, orders)
        packed = jnp.concatenate([mine[:, b, :, :, slot_count * b :] for b in range(buckets)], axis=-1)
        return packed.transpose(1, 0, 2, 3)

    def kernel(_, in_ref, out_ref):
        pieces = [
            in_ref[0, slot_count * b : slot_count * (b + 1), slot_count * b :] for b in range(buckets)
        ]
        rows = jnp.concatenate(pieces, axis=-1)
        for owner in range(owners):
            out_ref[owner, 0] = rows[owner * share : (owner + 1) * share]

    return pl.pallas_call(
        kernel,
        grid_spec=pltpu.PrefetchScalarGridSpec(
            num_scalar_prefetch=1,
            grid=(latitudes,),
            in_specs=[pl.BlockSpec((1, orders, orders), lambda t, g: (g[0] + t, 0, 0))],
            out_specs=pl.BlockSpec((owners, 1, share, lanes), lambda t, g: (0, t, 0, 0)),
        ),
        out_shape=jax.ShapeDtypeStruct((owners, latitudes, share, lanes), jnp.bfloat16),
        compiler_params=pltpu.CompilerParams(vmem_limit_bytes=VMEM_BYTES),
    )(jnp.reshape(group * latitudes, (1,)).astype(jnp.int32), legendre)


def local(coefficients, rotations, legendre, degree_slot, column_order):
    owners = lax.axis_size("own")
    groups = lax.axis_size("grp")
    own_index = lax.axis_index("own")
    slot_local, columns, _ = coefficients.shape
    buckets, slot_count = degree_slot.shape
    orders = slot_count * buckets
    longitudes = 2 * orders
    latitudes = legendre.shape[0]
    share = slot_count // owners

    shared = latitudes % groups == 0
    packed = pack(legendre, buckets, slot_count, owners, groups if shared else 1)
    lanes = packed.shape[-1]
    moved = lax.all_to_all(packed, "own", split_axis=0, concat_axis=0, tiled=True)

    degrees = lax.dynamic_slice_in_dim(degree_slot, own_index * slot_local, slot_local, axis=1)
    degrees = degrees + slot_count * jnp.arange(buckets, dtype=jnp.int32)[:, None]
    column_ids = jnp.arange(columns, dtype=jnp.int32)
    column_pick = (column_ids[:, None] == column_order[None, :]).astype(jnp.bfloat16)

    high = buckets - buckets // 4
    chunks = [list(range(buckets - 1, high - 1, -1)), list(range(high - 1, -1, -1))]
    received = {}
    for classes in chunks:
        rotated = rotate_classes(
            coefficients, rotations, degrees, column_pick, classes, slot_count, owners
        )
        outgoing = jnp.concatenate(
            [part.reshape(slot_local, owners, -1, columns) for part in rotated], axis=2
        ).transpose(1, 0, 2, 3)
        degrees, _ = lax.optimization_barrier((degrees, outgoing))
        arrived = lax.all_to_all(outgoing, "own", split_axis=0, concat_axis=0, tiled=True)
        arrived = arrived.reshape(owners * slot_local, -1, columns)
        start = 0
        for bucket in classes:
            size = (bucket + 1) * share * 2
            received[bucket] = arrived[:, start : start + size].reshape(
                owners * slot_local, bucket + 1, share, 2, columns
            )
            start += size

    if shared:
        moved = lax.all_gather(moved, "grp", axis=0, tiled=False)
        moved = moved.reshape(groups, owners, latitudes // groups, share, lanes)
        moved = moved.transpose(1, 0, 2, 3, 4)
    moved = moved.reshape(owners * latitudes, share, lanes)
    held_degrees = degree_slot + slot_count * jnp.arange(buckets, dtype=jnp.int32)[:, None]
    permuter = jnp.arange(orders, dtype=jnp.int32)[:, None] == held_degrees.reshape(1, -1)
    permuter = permuter.astype(jnp.bfloat16)
    tables_of_blocks = []
    for block in range(buckets):
        start = slot_count * (block * buckets - block * (block - 1) // 2)
        first = slot_count * block
        rows = jnp.einsum(
            "til,lj->itj",
            moved[:, :, start : start + orders - first],
            permuter[first:, first:],
            preferred_element_type=jnp.float32,
        )
        tables_of_blocks.append(rows.astype(jnp.bfloat16))
    low_arrived = {k: received[k] for k in chunks[1]}
    low_arrived, tables_of_blocks[:high] = lax.optimization_barrier(
        (low_arrived, tables_of_blocks[:high])
    )

    def synthesize(blocks, received, parts):
        pieces = []
        for block in blocks:
            values = jnp.concatenate([received[k][:, block] for k in range(block, buckets)], axis=0)
            summed = jnp.einsum(
                "itj,jipc->tipc", tables_of_blocks[block], values, preferred_element_type=jnp.float32
            )
            pieces.append(summed.astype(jnp.bfloat16).reshape(owners, latitudes, share * 2, columns))
        outgoing = jnp.concatenate(pieces, axis=2)
        if parts:
            outgoing, parts[-1] = lax.optimization_barrier((outgoing, parts[-1]))
        return lax.all_to_all(outgoing, "own", split_axis=0, concat_axis=0, tiled=True)

    longitude = jnp.arange(longitudes, dtype=jnp.int32)
    groups_of_blocks = [
        list(range(high, buckets)),
        list(range(high)),
    ]
    parts, tables = [], []
    received = {**received, **low_arrived}
    for blocks in groups_of_blocks:
        parts.append(synthesize(blocks, received, parts))
        held = (
            slot_count * jnp.asarray(blocks, jnp.int32)[None, :, None]
            + share * jnp.arange(owners, dtype=jnp.int32)[:, None, None]
            + jnp.arange(share, dtype=jnp.int32)[None, None, :]
        ).reshape(-1)
        product_mod = held[:, None] * longitude[None, :] % longitudes
        angles = product_mod.astype(jnp.float32) * (2.0 * math.pi / longitudes)
        table = jnp.stack([jnp.cos(angles), jnp.sin(angles)], axis=1) / orders
        tables.append(table.astype(jnp.bfloat16).reshape(-1, longitudes))
    return transform(parts, tables)


def solution(mesh):
    placed = (P("own", "grp", None), P("own", None), P("own", None, None), P(), P("grp"))
    return jax.shard_map(
        local, mesh=mesh, in_specs=placed, out_specs=P("grp", "own", None), check_vma=False
    )
```
